256 devices in a mesh: section: 8 (over z_lo, core), dp: 32 (over z_hi, x, y).
Axes of the slice: x: 4, y: 4, z: 8 (z_hi: 2, z_lo: 4; z = z_hi * 4 + z_lo), core: 2. Of those that a mesh axis runs over, the one named last changes fastest.
Arguments:
- acts: bfloat16 [16, 2, 32, 128, 4096], P('section', None, 'dp'), may hold values from -6 to 6
- gates: bfloat16 [16, 2, 32, 128, 4096], P('section', None, 'dp'), may hold values from -6 to 6
- filters: bfloat16 [16, 256, 128], P('section', 'dp'), may hold values from -0.15625 to 0.15625
- bases: bfloat16 [16, 4096, 128], P('section', 'dp'), may hold values from -0.09375 to 0.09375
- final_hidden: bfloat16 [2, 32, 128, 4096], P(None, 'dp'), may hold values from -40 to 40
- unembed: bfloat16 [4096, 512], P('dp'), may hold values from -0.09375 to 0.09375
- targets: int32 [2, 32, 128], P(None, 'dp'), may hold values from 0 to 511
Outputs:
- features: float32 [2, 32, 4096], P(None, 'dp')
The draws below stay inside these ranges and needn't reach their ends.
All inputs are finite; a program needn't handle non-finite values.
Results may differ from the reference program's by a relative error of at most 0.02.
Values may be sent and summed in bfloat16 or wider, within the bound.
No kernel may reach another device: no remote copies, remote signals or barrier semaphores. Data moves between devices by JAX's collectives and lax.ppermute only.
A program may use at most 128 MiB of HBM per device.

```python
import math
import jax
import jax.numpy as jnp
from jax import lax

D = 4096
V = 512
G = 256
K = 128
R = 64
L = 128
MICRO = 2
LAYERS = 16
SEQS = 32


def shared_vocab(key):
    weights = jax.random.normal(key, (D, V), jnp.float32) / math.sqrt(D)
    return jnp.clip(weights, -0.09375, 0.09375)


def draw_unembed(key, part):
    weights = shared_vocab(key)
    return weights.astype(jnp.bfloat16)


def draw_final_hidden(key, part):
    key = jax.random.fold_in(key, 12)
    keys = jax.random.split(key, 1)
    shape = (MICRO, SEQS, L)
    states = jax.random.normal(keys[0], shape + (D,), jnp.float32) * 3.0
    return jnp.clip(states, -40.0, 40.0).astype(jnp.bfloat16)


def set_ends(result, own_key, smallest, high):
    longest = result.shape.index(max(result.shape))
    spots = []
    for shift in (0, 1):
        where = [jax.random.randint(jax.random.fold_in(own_key, axis), (), 0, length) for axis, length in enumerate(result.shape)]
        where[longest] = (where[longest] + shift) % result.shape[longest]
        spots.append(tuple(where))
    return result.at[spots[0]].set(smallest).at[spots[1]].set(high)


def block_scale(rng, shape, pieces, least, high):
    factor_of = 1.0
    for dim, parts in pieces:
        steps = jax.random.uniform(jax.random.fold_in(jax.random.fold_in(rng, 6), dim), (parts,), jnp.float32, least / len(pieces), high / len(pieces))
        factor_of = factor_of * jnp.repeat(jnp.exp(steps), shape[dim] // parts).reshape((-1,) + (1,) * (len(shape) - 1 - dim))
    return factor_of


def scatter_about(own_key, dims, spread, limit, cuts=(), dtype=jnp.bfloat16):
    level = block_scale(own_key, dims, cuts, -0.22, 0.18) if cuts else 1.0
    drawn = jax.random.normal(own_key, dims, jnp.float32) * spread * level
    return jnp.minimum(jnp.maximum(drawn, -limit), limit).astype(dtype)


def setup_inputs(seed: int = 0) -> dict:
    splits = jax.random.split(jax.random.key(seed), 8)
    return {
        "acts": scatter_about(splits[0], (LAYERS, MICRO, SEQS, L, D), 1.0, 6.0, ((0, 8), (2, 32))),
        "gates": scatter_about(splits[1], (LAYERS, MICRO, SEQS, L, D), 1.0, 6.0, ((0, 8), (2, 32))),
        "filters": scatter_about(splits[2], (LAYERS, G, K), (10 * K) ** -0.5, 0.15625, ((0, 8), (1, 32))),
        "bases": scatter_about(splits[3], (LAYERS, D, 2 * R), D ** -0.5, 0.09375, ((0, 8), (1, 32))),
        "final_hidden": draw_final_hidden(jax.random.fold_in(splits[7], 71), 0),
        "unembed": draw_unembed(jax.random.fold_in(splits[7], 71), 0),
        "targets": set_ends(jax.random.randint(splits[6], (MICRO, SEQS, L), 0, V), jax.random.fold_in(splits[6], 1), 0, V - 1).astype(jnp.int32),
    }


def band_pair(kernel):
    taps = kernel.shape[1]
    offset = jnp.arange(taps)[None, :] - jnp.arange(taps)[:, None]
    within = jnp.where(offset[None] >= 0, kernel[:, jnp.clip(offset, 0, taps - 1)], 0.0)
    across = jnp.where(offset[None] < 0, kernel[:, jnp.clip(offset + taps, 0, taps - 1)], 0.0)
    return within, across


def spread_back(values, within, across):
    seq_len = values.shape[-2]
    model_dim = values.shape[-1]
    groups = within.shape[0]
    taps = within.shape[1]
    leading = values.shape[:-2]
    blocks = values.reshape(leading + (seq_len // taps, taps, groups, model_dim // groups))
    following = jnp.concatenate([blocks[..., 1:, :, :, :], jnp.zeros_like(blocks[..., :1, :, :, :])], axis=-4)
    summed = jnp.einsum("gtu,...bugc->...btgc", within, blocks) + jnp.einsum("gtu,...bugc->...btgc", across, following)
    return summed.reshape(values.shape)


def reference(acts, gates, filters, bases, final_hidden, unembed, targets):
    hidden_rows = final_hidden.reshape(-1, D)
    logits = jnp.dot(hidden_rows, unembed, preferred_element_type=jnp.float32)
    row_peak = jnp.max(logits, axis=1, keepdims=True)
    exp_terms = jnp.exp(logits - row_peak)
    probabilities = exp_terms / jnp.sum(exp_terms, axis=1, keepdims=True)
    onehot = (targets.reshape(-1)[:, None] == jnp.arange(V)[None, :]).astype(jnp.float32)
    dlogits = (probabilities - onehot).astype(jnp.bfloat16)
    cotangent = jnp.dot(dlogits, unembed.T, preferred_element_type=jnp.float32).astype(jnp.bfloat16)
    cotangent = cotangent.reshape(MICRO, SEQS, L, D)
    features = jnp.zeros((MICRO, SEQS, R * R), jnp.float32)
    for layer_no in reversed(range(LAYERS)):
        basis = bases[layer_no]
        rows_in = jnp.dot(acts[layer_no].reshape(-1, D), basis[:, :R], preferred_element_type=jnp.float32)
        rows_out = jnp.dot(cotangent.reshape(-1, D), basis[:, R:], preferred_element_type=jnp.float32)
        rows_in = rows_in.reshape(MICRO, SEQS, L, R)
        rows_out = rows_out.reshape(MICRO, SEQS, L, R)
        outer_sum = jnp.einsum("mslo,msli->msoi", rows_out, rows_in, precision=lax.Precision.HIGHEST)
        features = features + outer_sum.reshape(MICRO, SEQS, R * R)
        scaled = (gates[layer_no].astype(jnp.float32) * cotangent.astype(jnp.float32)).astype(jnp.bfloat16)
        scaled = lax.optimization_barrier(scaled)
        within, across = band_pair(filters[layer_no].astype(jnp.float32))
        back = spread_back(scaled.astype(jnp.float32), within, across)
        cotangent = (cotangent.astype(jnp.float32) + back).astype(jnp.bfloat16)
    return features
```

```python
import functools
import jax
import jax.numpy as jnp
from jax import lax
from jax.sharding import PartitionSpec as P
from jax.experimental import pallas as pl
from jax.experimental.pallas import tpu as pltpu

BF = jnp.bfloat16
F32 = jnp.float32
CHUNKS = 2
PIECES = ((0, 512), (512, 512))
VMEM = 16 * 1024 * 1024
PARAMS = dict(compiler_params=pltpu.CompilerParams(vmem_limit_bytes=VMEM))


def swap(value, axis, bit):
    count = lax.axis_size(axis)
    return lax.ppermute(value, axis, [(i, i ^ bit) for i in range(count)])


def after(value, *others):
    return lax.optimization_barrier((value, others))[0]


def whole(shape):
    return pl.BlockSpec(shape, lambda *ids: (0,) * len(shape))


def held(count):
    return [pl.BlockSpec(memory_space=pltpu.VMEM)] * count


def paired(ref, block):
    return jnp.concatenate(
        [ref[:, block * 256 : block * 256 + 256], ref[:, 2048 + block * 256 : 2304 + block * 256]], axis=1
    )


def sort_matrix(quarters):
    row = lax.broadcasted_iota(jnp.int32, (512, 128), 0)
    col = lax.broadcasted_iota(jnp.int32, (512, 128), 1)
    tile = (col // 32) % 2 * 2 + col // 64
    return jnp.concatenate([(row == tile * 128 + quarter * 32 + col % 32).astype(BF) for quarter in quarters], axis=1)


def gates_body(gate_ref, sort_ref, *outs):
    for block in range(8):
        picked = jnp.dot(paired(gate_ref, block), sort_ref[...], preferred_element_type=F32).astype(BF)
        for number in range(4):
            for piece, (start, size) in enumerate(PIECES):
                lane = block * 128 - start
                if 0 <= lane < size:
                    outs[number * 2 + piece][:, lane : lane + 128] = picked[:, number * 128 : number * 128 + 128]


def sort_gates(gates, matrix):
    sizes = [size for _ in range(4) for _, size in PIECES]
    return pl.pallas_call(
        gates_body,
        grid=(2,),
        in_specs=[pl.BlockSpec((256, 4096), lambda i: (i, 0)), whole((512, 512))],
        out_specs=[pl.BlockSpec((256, size), lambda i: (i, 0)) for size in sizes],
        out_shape=[jax.ShapeDtypeStruct((512, size), BF) for size in sizes],
        name="sort_gates",
        compiler_params=pltpu.CompilerParams(vmem_limit_bytes=56 * 1024 * 1024),
    )(gates, matrix)


def hidden_body(hidden_ref, sort_ref, out_ref):
    for block in range(8):
        out_ref[:, block * 128 : block * 128 + 128] = jnp.dot(
            paired(hidden_ref, block), sort_ref[...], preferred_element_type=F32
        ).astype(BF)


def pick_hidden(hidden, matrix):
    return pl.pallas_call(
        hidden_body,
        in_specs=held(2),
        out_specs=held(1)[0],
        out_shape=jax.ShapeDtypeStruct((256, 1024), BF),
        name="pick_hidden",
        **PARAMS,
    )(hidden, matrix)


def logits_body(place_ref, hidden_ref, vocab_ref, keep_ref, send_ref, total_ref):
    total = jnp.zeros((256, 512), F32)
    for block in range(4):
        weights = jnp.concatenate(
            [
                vocab_ref[block * 8 : block * 8 + 8, part * 32 : part * 32 + 32, :].reshape(256, 128)
                for part in range(4)
            ],
            axis=1,
        )
        total = total + jnp.dot(
            hidden_ref[:, block * 256 : block * 256 + 256], weights, preferred_element_type=F32
        )
    total_ref[...] = total
    core = place_ref[1]
    keep_ref[...] = total_ref[pl.ds(pl.multiple_of(core * 128, 128), 128), :]
    send_ref[...] = total_ref[pl.ds(pl.multiple_of((1 - core) * 128, 128), 128), :]


def partial_logits(place, hidden, gathered):
    return pl.pallas_call(
        logits_body,
        in_specs=[pl.BlockSpec(memory_space=pltpu.SMEM)] + held(2),
        out_specs=held(2),
        out_shape=[jax.ShapeDtypeStruct((128, 512), F32)] * 2,
        scratch_shapes=[pltpu.VMEM((256, 512), F32)],
        name="partial_logits",
        **PARAMS,
    )(place, hidden, gathered)


def top_body(dlogits_ref, vocab_ref, out_ref):
    total = jnp.zeros((256, 256), F32)
    for part in range(4):
        weights = vocab_ref[:, part * 32 : part * 32 + 32, :].reshape(256, 128)
        total = total + lax.dot_general(
            dlogits_ref[:, part * 128 : part * 128 + 128], weights, (((1,), (1,)), ((), ())), preferred_element_type=F32
        )
    out_ref[...] = total.astype(BF)


def top_cotangent(dlogits, gathered):
    return pl.pallas_call(
        top_body,
        grid=(4,),
        in_specs=[
            whole((256, 512)),
            pl.BlockSpec((8, 128, 128), lambda i: (i, 0, 0)),
        ],
        out_specs=pl.BlockSpec((256, 256), lambda i: (0, i)),
        out_shape=jax.ShapeDtypeStruct((256, 1024), BF),
        name="top_cotangent",
        **PARAMS,
    )(dlogits, gathered)


def toeplitz(row):
    spread = jnp.broadcast_to(row, (128, 128))
    turned = pltpu.roll(spread, 0, 1, stride=1, stride_axis=0)
    earlier = lax.broadcasted_iota(jnp.int32, (128, 128), 0)
    later = lax.broadcasted_iota(jnp.int32, (128, 128), 1)
    return jnp.where(later >= earlier, turned, 0.0).astype(BF)


def piece_of(chunk):
    return max(number for number, (start, _) in enumerate(PIECES) if start <= chunk * 1024 // CHUNKS)


def layer_step(layer, place, cot_ref, gate_refs, filt_ref, chunk, tiles):
    zx = (layer // 4) ^ place[0]
    cx = (layer // 2 % 2) ^ place[1]
    lane = lax.broadcasted_iota(jnp.int32, (128, 256), 1) % 128
    odd = lane // 16 % 2 == 1
    for tile in range(tiles):
        lanes = slice(tile * 128, tile * 128 + 128)
        inside = (chunk * tiles + tile) * 128 - PIECES[piece_of(chunk)][0]
        gate_lanes = slice(inside, inside + 128)
        scaled = []
        olds = []
        for micro in range(2):
            rows = pl.ds(pl.multiple_of(layer % 2 * 256 + micro * 128, 128), 128)
            near, side, over, cross = [ref[rows, gate_lanes] for ref in gate_refs]
            gate = jnp.where(zx == 0, jnp.where(cx == 0, near, side), jnp.where(cx == 0, over, cross))
            old = cot_ref[micro * 128 : micro * 128 + 128, lanes].astype(F32)
            olds.append(old)
            scaled.append((gate.astype(F32) * old).astype(BF))
        values = jnp.concatenate(scaled, axis=1)
        none = jnp.zeros_like(values)
        split = jnp.concatenate([jnp.where(odd, none, values), jnp.where(odd, values, none)], axis=0)
        kept = None
        for pair in range(4):
            first = (chunk * tiles + tile) * 8 + pair * 2
            band = jnp.concatenate(
                [toeplitz(filt_ref[layer, first : first + 1, :]), toeplitz(filt_ref[layer, first + 1 : first + 2, :])],
                axis=1,
            )
            back = jnp.dot(band, split, preferred_element_type=F32)
            kept = back if pair == 0 else jnp.where(lane // 32 == pair, back, kept)
        for micro in range(2):
            cot_ref[micro * 128 : micro * 128 + 128, lanes] = (
                olds[micro] + kept[:, micro * 128 : micro * 128 + 128]
            ).astype(BF)


def upper_body(chunk, width, place_ref, cot_ref, near, side, over, cross, filt_ref, out_ref):
    place = (place_ref[0], place_ref[1])
    out_ref[...] = cot_ref[:, chunk * width : chunk * width + width]

    def step(i, carry):
        layer_step(7 - i, place, out_ref, (near, side, over, cross), filt_ref, chunk, width // 128)
        return carry

    lax.fori_loop(0, 8, step, 0)


def lower_body(
    chunk, width, place_ref, top_ref, recv_ref, near, side, over, cross, filt_ref, basis_ref, out_ref, cot_ref
):
    place = (place_ref[0], place_ref[1])
    is_top = place_ref[2] == 1
    cot_ref[...] = jnp.where(is_top, top_ref[:, chunk * width : chunk * width + width], recv_ref[...])
    lane = lax.broadcasted_iota(jnp.int32, (256, 128), 1)

    def project(layer):
        slot = ((layer // 4) ^ place[0]) * 2 + ((layer // 2 % 2) ^ place[1])
        rows = pl.ds(pl.multiple_of(slot * 32, 32), 32)
        weights = basis_ref[chunk * (width // 32) : (chunk + 1) * (width // 32), rows, :].reshape(width, 128)
        made = jnp.dot(cot_ref[...], weights, preferred_element_type=F32)
        out_ref[slot] = jnp.where(lane // 64 == layer % 2, made, out_ref[slot])

    def step(i, carry):
        project(7 - i)
        layer_step(7 - i, place, cot_ref, (near, side, over, cross), filt_ref, chunk, width // 128)
        return carry

    out_ref[...] = jnp.zeros_like(out_ref)
    lax.fori_loop(0, 7, step, 0)
    project(0)


def upper(chunk, width, place, cot, gate_set, filt):
    return pl.pallas_call(
        functools.partial(upper_body, chunk, width),
        in_specs=[pl.BlockSpec(memory_space=pltpu.SMEM)] + held(6),
        out_specs=held(1)[0],
        out_shape=jax.ShapeDtypeStruct((256, width), BF),
        name="upper",
        **PARAMS,
    )(place, cot, *gate_set, filt)


def lower(chunk, width, place, cot, received, gate_set, filt, gathered):
    return pl.pallas_call(
        functools.partial(lower_body, chunk, width),
        in_specs=[pl.BlockSpec(memory_space=pltpu.SMEM)] + held(8),
        out_specs=held(1)[0],
        out_shape=jax.ShapeDtypeStruct((4, 256, 128), F32),
        scratch_shapes=[pltpu.VMEM((256, width), BF)],
        name="lower",
        **PARAMS,
    )(place, cot, received, *gate_set, filt, gathered)


def rows_in_body(acts_ref, basis_ref, out_ref):
    lane = lax.broadcasted_iota(jnp.int32, (256, 128), 1)
    made = []
    for layer in range(2):
        total = jnp.zeros((256, 128), F32)
        for block in range(16):
            left = acts_ref[layer, :, block * 128 : block * 128 + 128]
            right = acts_ref[layer, :, 2048 + block * 128 : 2176 + block * 128]
            weights = basis_ref[block * 2 : block * 2 + 2, 128:256, :].reshape(256, 128)
            total = total + jnp.dot(jnp.concatenate([left, right], axis=1), weights, preferred_element_type=F32)
        made.append(total)
    out_ref[...] = jnp.where(lane < 64, made[0], made[1])


def project_in(acts, gathered):
    return pl.pallas_call(
        rows_in_body,
        in_specs=held(2),
        out_specs=held(1)[0],
        out_shape=jax.ShapeDtypeStruct((256, 128), F32),
        name="rows_in",
        **PARAMS,
    )(acts, gathered)


def term_body(*refs):
    parts, rows_in_ref, out_ref = refs[:-2], refs[-2], refs[-1]
    for micro in range(2):
        rows = slice(micro * 128, micro * 128 + 128)
        total = jnp.zeros((128, 128), F32)
        for slot in range(4):
            rows_out = parts[0][slot, rows, :]
            for part in parts[1:]:
                rows_out = rows_out + part[slot, rows, :]
            total = total + lax.dot_general(
                rows_out,
                rows_in_ref[slot, rows, :],
                (((0,), (0,)), ((), ())),
                preferred_element_type=F32,
                precision=lax.Precision.HIGHEST,
            )
        out_ref[:, micro * 64 : micro * 64 + 64] = total[:64, :64] + total[64:, 64:]


def terms(parts, rows_in):
    return pl.pallas_call(
        term_body,
        in_specs=held(len(parts) + 1),
        out_specs=held(1)[0],
        out_shape=jax.ShapeDtypeStruct((64, 128), F32),
        name="terms",
        **PARAMS,
    )(*parts, rows_in)


def with_other(value):
    other = swap(value, "dp", 16)
    high = lax.axis_index("dp") // 16
    return jnp.where(high == 0, jnp.stack([value, other]), jnp.stack([other, value]))


def gather_xy(both):
    groups = [list(range(16)), list(range(16, 32))]
    spread = jnp.broadcast_to(both[None], (16,) + both.shape)
    out = lax.all_to_all(spread, "dp", 0, 0, axis_index_groups=groups)
    return out.reshape((32,) + both.shape[1:])


def shards(acts, gates, filters, bases, final_hidden, unembed, targets):
    section = lax.axis_index("section")
    core = section % 2
    zbit = section // 2 % 2
    place = jnp.stack([zbit, core, section // 4, section]).astype(jnp.int32)
    quarter = 2 * core + zbit

    def pick(value, index, count, axis=0):
        return lax.dynamic_slice_in_dim(value, index, count, axis)

    matrix = sort_matrix([quarter, 2 * core + 1 - zbit, 2 * (1 - core) + zbit, 2 * (1 - core) + 1 - zbit])
    gate_out = sort_gates(gates.reshape(512, 4096), matrix)
    near, far, side_send, cross_send = [gate_out[number * 2 : number * 2 + 2] for number in range(4)]
    unembed, bases, filters = after((unembed, bases, filters), gate_out)
    sides = [swap(value, "section", 1) for value in side_send]
    crosses = [swap(value, "section", 1) for value in cross_send]

    def vocab_rows(which):
        return pick(unembed, which * 32, 32).reshape(32, 4, 128).transpose(1, 0, 2).reshape(128, 128)

    high = lax.axis_index("dp") // 16
    mirror = [(s * 32 + d, (s ^ 6) * 32 + (d ^ 16)) for s in range(8) for d in range(32)]
    other = lax.ppermute(vocab_rows(2 * core + 1 - zbit), ("section", "dp"), mirror)
    mine = vocab_rows(quarter)
    vocab_both = jnp.where(high == 0, jnp.stack([mine, other]), jnp.stack([other, mine]))

    out_rows = jnp.concatenate([bases[0, :, 64:], bases[1, :, 64:]], axis=1).reshape(4, 32, 128)
    filt_rows = filters.reshape(2, 4, 2, 128).transpose(1, 0, 2, 3).reshape(4, 4, 128)
    small = jnp.concatenate([out_rows, filt_rows], axis=1)
    side = swap(pick(small, 2 * (1 - core), 2), "section", 1)
    chip = jnp.stack([pick(small, 2 * core, 2), side], axis=1)
    over = swap(pick(chip, 1 - zbit, 1)[0], "section", 2)
    slots = jnp.concatenate([pick(chip, zbit, 1)[0], over], axis=0)
    out_slots = slots[:, :32].reshape(128, 128)
    filt_slots = slots[:, 32:].reshape(16, 128)
    in_rows = jnp.concatenate([bases[0, :, :64], bases[1, :, :64]], axis=1)
    slots_both = with_other(jnp.concatenate([out_slots, in_rows, filt_slots], axis=0))

    hidden = pick_hidden(final_hidden.reshape(256, 4096), sort_matrix([quarter]))
    late = swap(far[1], "section", 2)
    vocab_both, slots_both, far, crosses, hidden, late = lax.optimization_barrier(
        (vocab_both, slots_both, far, crosses, hidden, late)
    )
    overs = [swap(far[0], "section", 2), late]
    crossed = [swap(crosses[0], "section", 2)]
    first = gather_xy(jnp.concatenate([vocab_both, slots_both[:, 256:]], axis=1))
    second = gather_xy(after(slots_both[:, :256], first))

    filt = first[:, 128:, :].astype(F32).reshape(32, 2, 2, 2, 2, 128)
    filt = jnp.where(zbit == 0, filt, filt[:, ::-1])
    filt = jnp.where(core == 0, filt, filt[:, :, ::-1])
    filt = filt.transpose(1, 2, 3, 0, 4, 5).reshape(8, 64, 128)

    keep, send = partial_logits(place, hidden, first)
    half = keep + swap(send, "section", 1)
    half = after(half, overs[0], crossed[0])
    rows = pick(half, zbit * 64, 64) + swap(pick(half, (1 - zbit) * 64, 64), "section", 2)
    ids = pick(targets.reshape(256), core * 128 + zbit * 64, 64)
    exps = jnp.exp(rows - jnp.max(rows, axis=1, keepdims=True))
    probs = exps / jnp.sum(exps, axis=1, keepdims=True)
    onehot = (ids[:, None] == jnp.arange(512)[None, :]).astype(F32)
    mine = (probs - onehot).astype(BF)
    other = swap(mine, "section", 2)
    crossed.append(swap(after(crosses[1], other), "section", 2))
    gate_sets = [(near[piece], sides[piece], overs[piece], crossed[piece]) for piece in range(2)]
    mine = jnp.where(zbit == 0, jnp.concatenate([mine, other]), jnp.concatenate([other, mine]))
    other = swap(mine, "section", 1)
    dlogits = jnp.where(core == 0, jnp.concatenate([mine, other]), jnp.concatenate([other, mine]))
    top = top_cotangent(dlogits, first)

    width = 1024 // CHUNKS
    received = []
    for chunk in range(CHUNKS):
        start = after(top, passed) if chunk else top
        passed = upper(chunk, width, place, start, gate_sets[piece_of(chunk)], filt)
        received.append(lax.ppermute(passed, "section", [(s, s - 4) for s in range(4, 8)]))

    start = after(received[0], passed)
    parts = [lower(0, width, place, top, start, gate_sets[0], filt, second)]
    rows_in = project_in(acts.reshape(2, 256, 4096), after(second, parts[0], received[1]))
    start = after(received[1], rows_in)
    parts.append(lower(1, width, place, top, start, gate_sets[1], filt, second))
    rows_in = jnp.stack([rows_in, swap(rows_in, "section", 1)])
    rows_in = jnp.concatenate([rows_in, swap(rows_in, "section", 2)], axis=0)
    feats = terms(parts, rows_in)
    feats = feats + swap(feats, "section", 1)
    feats = (feats + swap(feats, "section", 2)) + (swap(feats, "section", 4) + swap(feats, "section", 6))
    return feats.reshape(64, 2, 64).transpose(1, 0, 2).reshape(2, 1, 4096)


def solution(mesh):
    in_specs = (
        P("section", None, "dp", None, None),
        P("section", None, "dp", None, None),
        P("section", "dp", None),
        P("section", "dp", None),
        P(None, "dp", None, None),
        P("dp", None),
        P(None, "dp", None),
    )
    return jax.shard_map(shards, mesh=mesh, in_specs=in_specs, out_specs=P(None, "dp", None), check_vma=False)
```

```python
import functools
import jax
import jax.numpy as jnp
from jax import lax
from jax.sharding import PartitionSpec as P
from jax.experimental import pallas as pl
from jax.experimental.pallas import tpu as pltpu

BF = jnp.bfloat16
F32 = jnp.float32
CHUNKS = 2
PIECES = ((0, 512), (512, 512))
VMEM = 8 * 1024 * 1024
PARAMS = dict(compiler_params=pltpu.CompilerParams(vmem_limit_bytes=VMEM))


def swap(value, axis, bit):
    count = lax.axis_size(axis)
    return lax.ppermute(value, axis, [(i, i ^ bit) for i in range(count)])


def after(value, *others):
    return lax.optimization_barrier((value, others))[0]


def whole(shape):
    return pl.BlockSpec(shape, lambda *ids: (0,) * len(shape))


def held(count):
    return [pl.BlockSpec(memory_space=pltpu.VMEM)] * count


def paired(ref, block):
    return jnp.concatenate(
        [ref[:, block * 256 : block * 256 + 256], ref[:, 2048 + block * 256 : 2304 + block * 256]], axis=1
    )


def sort_matrix(quarters):
    row = lax.broadcasted_iota(jnp.int32, (512, 128), 0)
    col = lax.broadcasted_iota(jnp.int32, (512, 128), 1)
    tile = (col // 32) % 2 * 2 + col // 64
    return jnp.concatenate([(row == tile * 128 + quarter * 32 + col % 32).astype(BF) for quarter in quarters], axis=1)


def gates_body(gate_ref, sort_ref, *outs):
    for block in range(8):
        picked = jnp.dot(paired(gate_ref, block), sort_ref[...], preferred_element_type=F32).astype(BF)
        for number in range(4):
            for piece, (start, size) in enumerate(PIECES):
                lane = block * 128 - start
                if 0 <= lane < size:
                    outs[number * 2 + piece][:, lane : lane + 128] = picked[:, number * 128 : number * 128 + 128]


def sort_gates(gates, matrix):
    sizes = [size for _ in range(4) for _, size in PIECES]
    return pl.pallas_call(
        gates_body,
        grid=(2,),
        in_specs=[pl.BlockSpec((256, 4096), lambda i: (i, 0)), whole((512, 512))],
        out_specs=[pl.BlockSpec((256, size), lambda i: (i, 0)) for size in sizes],
        out_shape=[jax.ShapeDtypeStruct((512, size), BF) for size in sizes],
        name="sort_gates",
        compiler_params=pltpu.CompilerParams(vmem_limit_bytes=56 * 1024 * 1024),
    )(gates, matrix)


def hidden_body(hidden_ref, sort_ref, out_ref):
    for block in range(8):
        out_ref[:, block * 128 : block * 128 + 128] = jnp.dot(
            paired(hidden_ref, block), sort_ref[...], preferred_element_type=F32
        ).astype(BF)


def pick_hidden(hidden, matrix):
    return pl.pallas_call(
        hidden_body,
        in_specs=held(2),
        out_specs=held(1)[0],
        out_shape=jax.ShapeDtypeStruct((256, 1024), BF),
        name="pick_hidden",
        **PARAMS,
    )(hidden, matrix)


def logits_body(place_ref, hidden_ref, vocab_ref, keep_ref, send_ref, total_ref):
    total = jnp.zeros((256, 512), F32)
    for block in range(4):
        weights = jnp.concatenate(
            [
                vocab_ref[block * 8 : block * 8 + 8, part * 32 : part * 32 + 32, :].reshape(256, 128)
                for part in range(4)
            ],
            axis=1,
        )
        total = total + jnp.dot(
            hidden_ref[:, block * 256 : block * 256 + 256], weights, preferred_element_type=F32
        )
    total_ref[...] = total
    core = place_ref[1]
    keep_ref[...] = total_ref[pl.ds(pl.multiple_of(core * 128, 128), 128), :]
    send_ref[...] = total_ref[pl.ds(pl.multiple_of((1 - core) * 128, 128), 128), :]


def partial_logits(place, hidden, gathered):
    return pl.pallas_call(
        logits_body,
        in_specs=[pl.BlockSpec(memory_space=pltpu.SMEM)] + held(2),
        out_specs=held(2),
        out_shape=[jax.ShapeDtypeStruct((128, 512), F32)] * 2,
        scratch_shapes=[pltpu.VMEM((256, 512), F32)],
        name="partial_logits",
        **PARAMS,
    )(place, hidden, gathered)


def top_body(dlogits_ref, vocab_ref, out_ref):
    total = jnp.zeros((256, 256), F32)
    for part in range(4):
        weights = vocab_ref[:, part * 32 : part * 32 + 32, :].reshape(256, 128)
        total = total + lax.dot_general(
            dlogits_ref[:, part * 128 : part * 128 + 128], weights, (((1,), (1,)), ((), ())), preferred_element_type=F32
        )
    out_ref[...] = total.astype(BF)


def top_cotangent(dlogits, gathered):
    return pl.pallas_call(
        top_body,
        grid=(4,),
        in_specs=[
            whole((256, 512)),
            pl.BlockSpec((8, 128, 128), lambda i: (i, 0, 0)),
        ],
        out_specs=pl.BlockSpec((256, 256), lambda i: (0, i)),
        out_shape=jax.ShapeDtypeStruct((256, 1024), BF),
        name="top_cotangent",
        **PARAMS,
    )(dlogits, gathered)


def toeplitz(row):
    spread = jnp.broadcast_to(row, (128, 128))
    turned = pltpu.roll(spread, 0, 1, stride=1, stride_axis=0)
    earlier = lax.broadcasted_iota(jnp.int32, (128, 128), 0)
    later = lax.broadcasted_iota(jnp.int32, (128, 128), 1)
    return jnp.where(later >= earlier, turned, 0.0).astype(BF)


def piece_of(chunk):
    return max(number for number, (start, _) in enumerate(PIECES) if start <= chunk * 1024 // CHUNKS)


def layer_step(layer, place, cot_ref, gate_refs, filt_ref, chunk, tiles):
    zx = (layer // 4) ^ place[0]
    cx = (layer // 2 % 2) ^ place[1]
    lane = lax.broadcasted_iota(jnp.int32, (128, 256), 1) % 128
    odd = lane // 16 % 2 == 1
    for tile in range(tiles):
        lanes = slice(tile * 128, tile * 128 + 128)
        inside = (chunk * tiles + tile) * 128 - PIECES[piece_of(chunk)][0]
        gate_lanes = slice(inside, inside + 128)
        scaled = []
        olds = []
        for micro in range(2):
            rows = pl.ds(pl.multiple_of(layer % 2 * 256 + micro * 128, 128), 128)
            near, side, over, cross = [ref[rows, gate_lanes] for ref in gate_refs]
            gate = jnp.where(zx == 0, jnp.where(cx == 0, near, side), jnp.where(cx == 0, over, cross))
            old = cot_ref[micro * 128 : micro * 128 + 128, lanes].astype(F32)
            olds.append(old)
            scaled.append((gate.astype(F32) * old).astype(BF))
        values = jnp.concatenate(scaled, axis=1)
        none = jnp.zeros_like(values)
        split = jnp.concatenate([jnp.where(odd, none, values), jnp.where(odd, values, none)], axis=0)
        kept = None
        for pair in range(4):
            first = (chunk * tiles + tile) * 8 + pair * 2
            band = jnp.concatenate(
                [toeplitz(filt_ref[layer, first : first + 1, :]), toeplitz(filt_ref[layer, first + 1 : first + 2, :])],
                axis=1,
            )
            back = jnp.dot(band, split, preferred_element_type=F32)
            kept = back if pair == 0 else jnp.where(lane // 32 == pair, back, kept)
        for micro in range(2):
            cot_ref[micro * 128 : micro * 128 + 128, lanes] = (
                olds[micro] + kept[:, micro * 128 : micro * 128 + 128]
            ).astype(BF)


def upper_body(chunk, width, place_ref, cot_ref, near, side, over, cross, filt_ref, out_ref):
    place = (place_ref[0], place_ref[1])
    out_ref[...] = cot_ref[:, chunk * width : chunk * width + width]

    def step(i, carry):
        layer_step(7 - i, place, out_ref, (near, side, over, cross), filt_ref, chunk, width // 128)
        return carry

    lax.fori_loop(0, 8, step, 0)


def lower_body(
    chunk, width, place_ref, top_ref, recv_ref, near, side, over, cross, filt_ref, basis_ref, out_ref, cot_ref
):
    place = (place_ref[0], place_ref[1])
    is_top = place_ref[2] == 1
    cot_ref[...] = jnp.where(is_top, top_ref[:, chunk * width : chunk * width + width], recv_ref[...])
    lane = lax.broadcasted_iota(jnp.int32, (256, 128), 1)

    def project(layer):
        slot = ((layer // 4) ^ place[0]) * 2 + ((layer // 2 % 2) ^ place[1])
        rows = pl.ds(pl.multiple_of(slot * 32, 32), 32)
        weights = basis_ref[chunk * (width // 32) : (chunk + 1) * (width // 32), rows, :].reshape(width, 128)
        made = jnp.dot(cot_ref[...], weights, preferred_element_type=F32)
        out_ref[slot] = jnp.where(lane // 64 == layer % 2, made, out_ref[slot])

    def step(i, carry):
        project(7 - i)
        layer_step(7 - i, place, cot_ref, (near, side, over, cross), filt_ref, chunk, width // 128)
        return carry

    out_ref[...] = jnp.zeros_like(out_ref)
    lax.fori_loop(0, 7, step, 0)
    project(0)


def upper(chunk, width, place, cot, gate_set, filt):
    return pl.pallas_call(
        functools.partial(upper_body, chunk, width),
        in_specs=[pl.BlockSpec(memory_space=pltpu.SMEM)] + held(6),
        out_specs=held(1)[0],
        out_shape=jax.ShapeDtypeStruct((256, width), BF),
        name="upper",
        **PARAMS,
    )(place, cot, *gate_set, filt)


def lower(chunk, width, place, cot, received, gate_set, filt, gathered):
    return pl.pallas_call(
        functools.partial(lower_body, chunk, width),
        in_specs=[pl.BlockSpec(memory_space=pltpu.SMEM)] + held(8),
        out_specs=held(1)[0],
        out_shape=jax.ShapeDtypeStruct((4, 256, 128), F32),
        scratch_shapes=[pltpu.VMEM((256, width), BF)],
        name="lower",
        **PARAMS,
    )(place, cot, received, *gate_set, filt, gathered)


def rows_in_body(stored_ref, basis_ref, out_ref, acts_ref, done):
    copies = [pltpu.make_async_copy(stored_ref.at[layer], acts_ref.at[layer], done.at[layer]) for layer in range(2)]
    for copy in copies:
        copy.start()
    lane = lax.broadcasted_iota(jnp.int32, (256, 128), 1)
    made = []
    for layer in range(2):
        copies[layer].wait()
        total = jnp.zeros((256, 128), F32)
        for block in range(16):
            left = acts_ref[layer, :, block * 128 : block * 128 + 128]
            right = acts_ref[layer, :, 2048 + block * 128 : 2176 + block * 128]
            weights = basis_ref[block * 2 : block * 2 + 2, 128:256, :].reshape(256, 128)
            total = total + jnp.dot(jnp.concatenate([left, right], axis=1), weights, preferred_element_type=F32)
        made.append(total)
    out_ref[...] = jnp.where(lane < 64, made[0], made[1])


def project_in(acts, gathered):
    return pl.pallas_call(
        rows_in_body,
        in_specs=[pl.BlockSpec(memory_space=pltpu.HBM)] + held(1),
        out_specs=held(1)[0],
        out_shape=jax.ShapeDtypeStruct((256, 128), F32),
        scratch_shapes=[pltpu.VMEM((2, 256, 4096), BF), pltpu.SemaphoreType.DMA((2,))],
        name="rows_in",
        **PARAMS,
    )(acts, gathered)


def term_body(*refs):
    parts, rows_in, out_ref = refs[:-5], refs[-5:-1], refs[-1]
    for micro in range(2):
        rows = slice(micro * 128, micro * 128 + 128)
        total = jnp.zeros((128, 128), F32)
        for slot in range(4):
            rows_out = parts[0][slot, rows, :]
            for part in parts[1:]:
                rows_out = rows_out + part[slot, rows, :]
            total = total + lax.dot_general(
                rows_out,
                rows_in[slot][rows, :].astype(F32),
                (((0,), (0,)), ((), ())),
                preferred_element_type=F32,
                precision=lax.Precision.HIGHEST,
            )
        out_ref[:, micro * 64 : micro * 64 + 64] = total[:64, :64] + total[64:, 64:]


def terms(parts, rows_in):
    return pl.pallas_call(
        term_body,
        in_specs=held(len(parts) + 4),
        out_specs=held(1)[0],
        out_shape=jax.ShapeDtypeStruct((64, 128), F32),
        name="terms",
        **PARAMS,
    )(*parts, *rows_in)


def with_other(value):
    other = swap(value, "dp", 16)
    high = lax.axis_index("dp") // 16
    return jnp.where(high == 0, jnp.stack([value, other]), jnp.stack([other, value]))


def gather_xy(both):
    groups = [list(range(16)), list(range(16, 32))]
    spread = jnp.broadcast_to(both[None], (16,) + both.shape)
    out = lax.all_to_all(spread, "dp", 0, 0, axis_index_groups=groups)
    return out.reshape((32,) + both.shape[1:])


def shards(acts, gates, filters, bases, final_hidden, unembed, targets):
    section = lax.axis_index("section")
    core = section % 2
    zbit = section // 2 % 2
    place = jnp.stack([zbit, core, section // 4, section]).astype(jnp.int32)
    quarter = 2 * core + zbit

    def pick(value, index, count, axis=0):
        return lax.dynamic_slice_in_dim(value, index, count, axis)

    matrix = sort_matrix([quarter, 2 * core + 1 - zbit, 2 * (1 - core) + zbit, 2 * (1 - core) + 1 - zbit])
    gate_out = sort_gates(gates.reshape(512, 4096), matrix)
    near, far, side_send, cross_send = [gate_out[number * 2 : number * 2 + 2] for number in range(4)]
    unembed, bases, filters = after((unembed, bases, filters), gate_out)
    sides = [swap(value, "section", 1) for value in side_send]
    crosses = [swap(value, "section", 1) for value in cross_send]

    def vocab_rows(which):
        return pick(unembed, which * 32, 32).reshape(32, 4, 128).transpose(1, 0, 2).reshape(128, 128)

    high = lax.axis_index("dp") // 16
    mirror = [(s * 32 + d, (s ^ 6) * 32 + (d ^ 16)) for s in range(8) for d in range(32)]
    other = lax.ppermute(vocab_rows(2 * core + 1 - zbit), ("section", "dp"), mirror)
    mine = vocab_rows(quarter)
    vocab_both = jnp.where(high == 0, jnp.stack([mine, other]), jnp.stack([other, mine]))

    out_rows = jnp.concatenate([bases[0, :, 64:], bases[1, :, 64:]], axis=1).reshape(4, 32, 128)
    filt_rows = filters.reshape(2, 4, 2, 128).transpose(1, 0, 2, 3).reshape(4, 4, 128)
    small = jnp.concatenate([out_rows, filt_rows], axis=1)
    side = swap(pick(small, 2 * (1 - core), 2), "section", 1)
    chip = jnp.stack([pick(small, 2 * core, 2), side], axis=1)
    over = swap(pick(chip, 1 - zbit, 1)[0], "section", 2)
    slots = jnp.concatenate([pick(chip, zbit, 1)[0], over], axis=0)
    out_slots = slots[:, :32].reshape(128, 128)
    filt_slots = slots[:, 32:].reshape(16, 128)
    in_rows = jnp.concatenate([bases[0, :, :64], bases[1, :, :64]], axis=1)
    slots_both = with_other(jnp.concatenate([out_slots, in_rows, filt_slots], axis=0))

    hidden = pick_hidden(final_hidden.reshape(256, 4096), sort_matrix([quarter]))
    late = swap(far[1], "section", 2)
    vocab_both, slots_both, far, crosses, hidden, late = lax.optimization_barrier(
        (vocab_both, slots_both, far, crosses, hidden, late)
    )
    overs = [swap(far[0], "section", 2), late]
    crossed = [swap(crosses[0], "section", 2)]
    first = gather_xy(jnp.concatenate([vocab_both, slots_both[:, 256:]], axis=1))
    second = gather_xy(after(slots_both[:, :256], first))

    filt = first[:, 128:, :].astype(F32).reshape(32, 2, 2, 2, 2, 128)
    filt = jnp.where(zbit == 0, filt, filt[:, ::-1])
    filt = jnp.where(core == 0, filt, filt[:, :, ::-1])
    filt = filt.transpose(1, 2, 3, 0, 4, 5).reshape(8, 64, 128)

    keep, send = partial_logits(place, hidden, first)
    half = keep + swap(send, "section", 1)
    half = after(half, overs[0], crossed[0])
    rows = pick(half, zbit * 64, 64) + swap(pick(half, (1 - zbit) * 64, 64), "section", 2)
    ids = pick(targets.reshape(256), core * 128 + zbit * 64, 64)
    exps = jnp.exp(rows - jnp.max(rows, axis=1, keepdims=True))
    probs = exps / jnp.sum(exps, axis=1, keepdims=True)
    onehot = (ids[:, None] == jnp.arange(512)[None, :]).astype(F32)
    mine = (probs - onehot).astype(BF)
    other = swap(mine, "section", 2)
    crossed.append(swap(after(crosses[1], other), "section", 2))
    gate_sets = [(near[piece], sides[piece], overs[piece], crossed[piece]) for piece in range(2)]
    mine = jnp.where(zbit == 0, jnp.concatenate([mine, other]), jnp.concatenate([other, mine]))
    other = swap(mine, "section", 1)
    dlogits = jnp.where(core == 0, jnp.concatenate([mine, other]), jnp.concatenate([other, mine]))
    top = top_cotangent(dlogits, first)

    width = 1024 // CHUNKS
    passed = upper(0, width, place, top, gate_sets[0], filt)
    down = [(s, s - 4) for s in range(4, 8)]
    received = [lax.ppermute(passed, "section", down)]
    rows_in = project_in(acts.reshape(2, 256, 4096), after(second, passed))
    passed = upper(1, width, place, after(top, rows_in), gate_sets[1], filt)
    received.append(lax.ppermute(passed, "section", down))
    sent = rows_in.astype(BF)
    rows_in = [rows_in] + [swap(sent, "section", bit) for bit in (1, 2, 3)]

    parts = [lower(0, width, place, top, after(received[0], passed), gate_sets[0], filt, second)]
    start = after(received[1], parts[0])
    parts.append(lower(1, width, place, top, start, gate_sets[1], filt, second))
    feats = terms(parts, rows_in)
    feats = feats + swap(feats, "section", 1)
    feats = (feats + swap(feats, "section", 2)) + (swap(feats, "section", 4) + swap(feats, "section", 6))
    return feats.reshape(64, 2, 64).transpose(1, 0, 2).reshape(2, 1, 4096)


def solution(mesh):
    in_specs = (
        P("section", None, "dp", None, None),
        P("section", None, "dp", None, None),
        P("section", "dp", None),
        P("section", "dp", None),
        P(None, "dp", None, None),
        P("dp", None),
        P(None, "dp", None),
    )
    return jax.shard_map(shards, mesh=mesh, in_specs=in_specs, out_specs=P(None, "dp", None), check_vma=False)
```

```python
import functools
import jax
import jax.numpy as jnp
from jax import lax
from jax.sharding import PartitionSpec as P
from jax.experimental import pallas as pl
from jax.experimental.pallas import tpu as pltpu

BF = jnp.bfloat16
F32 = jnp.float32
CHUNKS = 2
PIECES = ((0, 512), (512, 512))
VMEM = 8 * 1024 * 1024
PARAMS = dict(compiler_params=pltpu.CompilerParams(vmem_limit_bytes=VMEM))


def swap(value, axis, bit):
    count = lax.axis_size(axis)
    return lax.ppermute(value, axis, [(i, i ^ bit) for i in range(count)])


def after(value, *others):
    return lax.optimization_barrier((value, others))[0]


def whole(shape):
    return pl.BlockSpec(shape, lambda *ids: (0,) * len(shape))


def held(count):
    return [pl.BlockSpec(memory_space=pltpu.VMEM)] * count


def paired(ref, block):
    return jnp.concatenate(
        [ref[:, block * 256 : block * 256 + 256], ref[:, 2048 + block * 256 : 2304 + block * 256]], axis=1
    )


def sort_matrix(quarters):
    row = lax.broadcasted_iota(jnp.int32, (512, 128), 0)
    col = lax.broadcasted_iota(jnp.int32, (512, 128), 1)
    tile = (col // 32) % 2 * 2 + col // 64
    return jnp.concatenate([(row == tile * 128 + quarter * 32 + col % 32).astype(BF) for quarter in quarters], axis=1)


def gates_body(gate_ref, sort_ref, *outs):
    for block in range(8):
        picked = jnp.dot(paired(gate_ref, block), sort_ref[...], preferred_element_type=F32).astype(BF)
        for number in range(4):
            for piece, (start, size) in enumerate(PIECES):
                lane = block * 128 - start
                if 0 <= lane < size:
                    outs[number * 2 + piece][:, lane : lane + 128] = picked[:, number * 128 : number * 128 + 128]


def sort_gates(gates, matrix):
    sizes = [size for _ in range(4) for _, size in PIECES]
    return pl.pallas_call(
        gates_body,
        grid=(2,),
        in_specs=[pl.BlockSpec((256, 4096), lambda i: (i, 0)), whole((512, 512))],
        out_specs=[pl.BlockSpec((256, size), lambda i: (i, 0)) for size in sizes],
        out_shape=[jax.ShapeDtypeStruct((512, size), BF) for size in sizes],
        name="sort_gates",
        compiler_params=pltpu.CompilerParams(vmem_limit_bytes=56 * 1024 * 1024),
    )(gates, matrix)


def hidden_body(hidden_ref, sort_ref, out_ref):
    for block in range(8):
        out_ref[:, block * 128 : block * 128 + 128] = jnp.dot(
            paired(hidden_ref, block), sort_ref[...], preferred_element_type=F32
        ).astype(BF)


def pick_hidden(hidden, matrix):
    return pl.pallas_call(
        hidden_body,
        in_specs=held(2),
        out_specs=held(1)[0],
        out_shape=jax.ShapeDtypeStruct((256, 1024), BF),
        name="pick_hidden",
        **PARAMS,
    )(hidden, matrix)


def logits_body(place_ref, hidden_ref, vocab_ref, keep_ref, send_ref, total_ref):
    total = jnp.zeros((256, 512), F32)
    for block in range(4):
        weights = jnp.concatenate(
            [
                vocab_ref[block * 8 : block * 8 + 8, part * 32 : part * 32 + 32, :].reshape(256, 128)
                for part in range(4)
            ],
            axis=1,
        )
        total = total + jnp.dot(
            hidden_ref[:, block * 256 : block * 256 + 256], weights, preferred_element_type=F32
        )
    total_ref[...] = total
    core = place_ref[1]
    keep_ref[...] = total_ref[pl.ds(pl.multiple_of(core * 128, 128), 128), :]
    send_ref[...] = total_ref[pl.ds(pl.multiple_of((1 - core) * 128, 128), 128), :]


def partial_logits(place, hidden, gathered):
    return pl.pallas_call(
        logits_body,
        in_specs=[pl.BlockSpec(memory_space=pltpu.SMEM)] + held(2),
        out_specs=held(2),
        out_shape=[jax.ShapeDtypeStruct((128, 512), F32)] * 2,
        scratch_shapes=[pltpu.VMEM((256, 512), F32)],
        name="partial_logits",
        **PARAMS,
    )(place, hidden, gathered)


def top_body(dlogits_ref, vocab_ref, out_ref):
    total = jnp.zeros((256, 256), F32)
    for part in range(4):
        weights = vocab_ref[:, part * 32 : part * 32 + 32, :].reshape(256, 128)
        total = total + lax.dot_general(
            dlogits_ref[:, part * 128 : part * 128 + 128], weights, (((1,), (1,)), ((), ())), preferred_element_type=F32
        )
    out_ref[...] = total.astype(BF)


def top_cotangent(dlogits, gathered):
    return pl.pallas_call(
        top_body,
        grid=(4,),
        in_specs=[
            whole((256, 512)),
            pl.BlockSpec((8, 128, 128), lambda i: (i, 0, 0)),
        ],
        out_specs=pl.BlockSpec((256, 256), lambda i: (0, i)),
        out_shape=jax.ShapeDtypeStruct((256, 1024), BF),
        name="top_cotangent",
        **PARAMS,
    )(dlogits, gathered)


def toeplitz(row):
    spread = jnp.broadcast_to(row, (128, 128))
    turned = pltpu.roll(spread, 0, 1, stride=1, stride_axis=0)
    earlier = lax.broadcasted_iota(jnp.int32, (128, 128), 0)
    later = lax.broadcasted_iota(jnp.int32, (128, 128), 1)
    return jnp.where(later >= earlier, turned, 0.0).astype(BF)


def piece_of(chunk):
    return max(number for number, (start, _) in enumerate(PIECES) if start <= chunk * 1024 // CHUNKS)


def layer_step(layer, place, cot_ref, gate_refs, filt_ref, chunk, tiles):
    zx = (layer // 4) ^ place[0]
    cx = (layer // 2 % 2) ^ place[1]
    lane = lax.broadcasted_iota(jnp.int32, (128, 256), 1) % 128
    odd = lane // 16 % 2 == 1
    for tile in range(tiles):
        lanes = slice(tile * 128, tile * 128 + 128)
        inside = (chunk * tiles + tile) * 128 - PIECES[piece_of(chunk)][0]
        gate_lanes = slice(inside, inside + 128)
        scaled = []
        olds = []
        for micro in range(2):
            rows = pl.ds(pl.multiple_of(layer % 2 * 256 + micro * 128, 128), 128)
            near, side, over, cross = [ref[rows, gate_lanes] for ref in gate_refs]
            gate = jnp.where(zx == 0, jnp.where(cx == 0, near, side), jnp.where(cx == 0, over, cross))
            old = cot_ref[micro * 128 : micro * 128 + 128, lanes].astype(F32)
            olds.append(old)
            scaled.append((gate.astype(F32) * old).astype(BF))
        values = jnp.concatenate(scaled, axis=1)
        none = jnp.zeros_like(values)
        split = jnp.concatenate([jnp.where(odd, none, values), jnp.where(odd, values, none)], axis=0)
        kept = None
        for pair in range(4):
            first = (chunk * tiles + tile) * 8 + pair * 2
            band = jnp.concatenate(
                [toeplitz(filt_ref[layer, first : first + 1, :]), toeplitz(filt_ref[layer, first + 1 : first + 2, :])],
                axis=1,
            )
            back = jnp.dot(band, split, preferred_element_type=F32)
            kept = back if pair == 0 else jnp.where(lane // 32 == pair, back, kept)
        for micro in range(2):
            cot_ref[micro * 128 : micro * 128 + 128, lanes] = (
                olds[micro] + kept[:, micro * 128 : micro * 128 + 128]
            ).astype(BF)


def upper_body(chunk, width, place_ref, cot_ref, near, side, over, cross, filt_ref, out_ref):
    place = (place_ref[0], place_ref[1])
    out_ref[...] = cot_ref[:, chunk * width : chunk * width + width]

    def step(i, carry):
        layer_step(7 - i, place, out_ref, (near, side, over, cross), filt_ref, chunk, width // 128)
        return carry

    lax.fori_loop(0, 8, step, 0)


def lower_body(
    chunk, width, place_ref, top_ref, recv_ref, near, side, over, cross, filt_ref, basis_ref, out_ref, cot_ref
):
    place = (place_ref[0], place_ref[1])
    is_top = place_ref[2] == 1
    cot_ref[...] = jnp.where(is_top, top_ref[:, chunk * width : chunk * width + width], recv_ref[...])
    lane = lax.broadcasted_iota(jnp.int32, (256, 128), 1)

    def project(layer):
        slot = ((layer // 4) ^ place[0]) * 2 + ((layer // 2 % 2) ^ place[1])
        rows = pl.ds(pl.multiple_of(slot * 32, 32), 32)
        weights = basis_ref[chunk * (width // 32) : (chunk + 1) * (width // 32), rows, :].reshape(width, 128)
        made = jnp.dot(cot_ref[...], weights, preferred_element_type=F32)
        out_ref[slot] = jnp.where(lane // 64 == layer % 2, made, out_ref[slot])

    def step(i, carry):
        project(7 - i)
        layer_step(7 - i, place, cot_ref, (near, side, over, cross), filt_ref, chunk, width // 128)
        return carry

    out_ref[...] = jnp.zeros_like(out_ref)
    lax.fori_loop(0, 7, step, 0)
    project(0)


def upper(chunk, width, place, cot, gate_set, filt):
    return pl.pallas_call(
        functools.partial(upper_body, chunk, width),
        in_specs=[pl.BlockSpec(memory_space=pltpu.SMEM)] + held(6),
        out_specs=held(1)[0],
        out_shape=jax.ShapeDtypeStruct((256, width), BF),
        name="upper",
        **PARAMS,
    )(place, cot, *gate_set, filt)


def lower(chunk, width, place, cot, received, gate_set, filt, gathered):
    return pl.pallas_call(
        functools.partial(lower_body, chunk, width),
        in_specs=[pl.BlockSpec(memory_space=pltpu.SMEM)] + held(8),
        out_specs=held(1)[0],
        out_shape=jax.ShapeDtypeStruct((4, 256, 128), F32),
        scratch_shapes=[pltpu.VMEM((256, width), BF)],
        name="lower",
        **PARAMS,
    )(place, cot, received, *gate_set, filt, gathered)


def rows_in_body(acts_ref, basis_ref, out_ref):
    lane = lax.broadcasted_iota(jnp.int32, (256, 128), 1)
    made = []
    for layer in range(2):
        total = jnp.zeros((256, 128), F32)
        for block in range(16):
            left = acts_ref[layer, :, block * 128 : block * 128 + 128]
            right = acts_ref[layer, :, 2048 + block * 128 : 2176 + block * 128]
            weights = basis_ref[block * 2 : block * 2 + 2, 128:256, :].reshape(256, 128)
            total = total + jnp.dot(jnp.concatenate([left, right], axis=1), weights, preferred_element_type=F32)
        made.append(total)
    out_ref[...] = jnp.where(lane < 64, made[0], made[1])


def project_in(acts, gathered):
    return pl.pallas_call(
        rows_in_body,
        in_specs=held(2),
        out_specs=held(1)[0],
        out_shape=jax.ShapeDtypeStruct((256, 128), F32),
        name="rows_in",
        **PARAMS,
    )(acts, gathered)


def term_body(*refs):
    parts, rows_in, out_ref = refs[:-5], refs[-5:-1], refs[-1]
    for micro in range(2):
        rows = slice(micro * 128, micro * 128 + 128)
        total = jnp.zeros((128, 128), F32)
        for slot in range(4):
            rows_out = parts[0][slot, rows, :]
            for part in parts[1:]:
                rows_out = rows_out + part[slot, rows, :]
            total = total + lax.dot_general(
                rows_out,
                rows_in[slot][rows, :].astype(F32),
                (((0,), (0,)), ((), ())),
                preferred_element_type=F32,
                precision=lax.Precision.HIGHEST,
            )
        out_ref[:, micro * 64 : micro * 64 + 64] = total[:64, :64] + total[64:, 64:]


def terms(parts, rows_in):
    return pl.pallas_call(
        term_body,
        in_specs=held(len(parts) + 4),
        out_specs=held(1)[0],
        out_shape=jax.ShapeDtypeStruct((64, 128), F32),
        name="terms",
        **PARAMS,
    )(*parts, *rows_in)


def with_other(value):
    other = swap(value, "dp", 16)
    high = lax.axis_index("dp") // 16
    return jnp.where(high == 0, jnp.stack([value, other]), jnp.stack([other, value]))


def gather_xy(both):
    groups = [list(range(16)), list(range(16, 32))]
    spread = jnp.broadcast_to(both[None], (16,) + both.shape)
    out = lax.all_to_all(spread, "dp", 0, 0, axis_index_groups=groups)
    return out.reshape((32,) + both.shape[1:])


def shards(acts, gates, filters, bases, final_hidden, unembed, targets):
    section = lax.axis_index("section")
    core = section % 2
    zbit = section // 2 % 2
    place = jnp.stack([zbit, core, section // 4, section]).astype(jnp.int32)
    quarter = 2 * core + zbit

    def pick(value, index, count, axis=0):
        return lax.dynamic_slice_in_dim(value, index, count, axis)

    matrix = sort_matrix([quarter, 2 * core + 1 - zbit, 2 * (1 - core) + zbit, 2 * (1 - core) + 1 - zbit])
    gate_out = sort_gates(gates.reshape(512, 4096), matrix)
    near, far, side_send, cross_send = [gate_out[number * 2 : number * 2 + 2] for number in range(4)]
    unembed, bases, filters = after((unembed, bases, filters), gate_out)
    sides = [swap(value, "section", 1) for value in side_send]
    crosses = [swap(value, "section", 1) for value in cross_send]

    def vocab_rows(which):
        return pick(unembed, which * 32, 32).reshape(32, 4, 128).transpose(1, 0, 2).reshape(128, 128)

    high = lax.axis_index("dp") // 16
    mirror = [(s * 32 + d, (s ^ 6) * 32 + (d ^ 16)) for s in range(8) for d in range(32)]
    other = lax.ppermute(vocab_rows(2 * core + 1 - zbit), ("section", "dp"), mirror)
    mine = vocab_rows(quarter)
    vocab_both = jnp.where(high == 0, jnp.stack([mine, other]), jnp.stack([other, mine]))

    out_rows = jnp.concatenate([bases[0, :, 64:], bases[1, :, 64:]], axis=1).reshape(4, 32, 128)
    filt_rows = filters.reshape(2, 4, 2, 128).transpose(1, 0, 2, 3).reshape(4, 4, 128)
    small = jnp.concatenate([out_rows, filt_rows], axis=1)
    side = swap(pick(small, 2 * (1 - core), 2), "section", 1)
    chip = jnp.stack([pick(small, 2 * core, 2), side], axis=1)
    over = swap(pick(chip, 1 - zbit, 1)[0], "section", 2)
    slots = jnp.concatenate([pick(chip, zbit, 1)[0], over], axis=0)
    out_slots = slots[:, :32].reshape(128, 128)
    filt_slots = slots[:, 32:].reshape(16, 128)
    in_rows = jnp.concatenate([bases[0, :, :64], bases[1, :, :64]], axis=1)
    slots_both = with_other(jnp.concatenate([out_slots, in_rows, filt_slots], axis=0))

    hidden = pick_hidden(final_hidden.reshape(256, 4096), sort_matrix([quarter]))
    late = swap(far[1], "section", 2)
    vocab_both, slots_both, far, crosses, hidden, late = lax.optimization_barrier(
        (vocab_both, slots_both, far, crosses, hidden, late)
    )
    overs = [swap(far[0], "section", 2), late]
    crossed = [swap(crosses[0], "section", 2)]
    first = gather_xy(jnp.concatenate([vocab_both, slots_both[:, 256:]], axis=1))
    second = gather_xy(after(slots_both[:, :256], first))

    filt = first[:, 128:, :].astype(F32).reshape(32, 2, 2, 2, 2, 128)
    filt = jnp.where(zbit == 0, filt, filt[:, ::-1])
    filt = jnp.where(core == 0, filt, filt[:, :, ::-1])
    filt = filt.transpose(1, 2, 3, 0, 4, 5).reshape(8, 64, 128)

    keep, send = partial_logits(place, hidden, first)
    half = keep + swap(send, "section", 1)
    half = after(half, overs[0], crossed[0])
    rows = pick(half, zbit * 64, 64) + swap(pick(half, (1 - zbit) * 64, 64), "section", 2)
    ids = pick(targets.reshape(256), core * 128 + zbit * 64, 64)
    exps = jnp.exp(rows - jnp.max(rows, axis=1, keepdims=True))
    probs = exps / jnp.sum(exps, axis=1, keepdims=True)
    onehot = (ids[:, None] == jnp.arange(512)[None, :]).astype(F32)
    mine = (probs - onehot).astype(BF)
    other = swap(mine, "section", 2)
    crossed.append(swap(after(crosses[1], other), "section", 2))
    gate_sets = [(near[piece], sides[piece], overs[piece], crossed[piece]) for piece in range(2)]
    mine = jnp.where(zbit == 0, jnp.concatenate([mine, other]), jnp.concatenate([other, mine]))
    other = swap(mine, "section", 1)
    dlogits = jnp.where(core == 0, jnp.concatenate([mine, other]), jnp.concatenate([other, mine]))
    top = top_cotangent(dlogits, first)

    width = 1024 // CHUNKS
    passed = upper(0, width, place, top, gate_sets[0], filt)
    down = [(s, s - 4) for s in range(4, 8)]
    received = [lax.ppermute(passed, "section", down)]
    rows_in = project_in(acts.reshape(2, 256, 4096), after(second, passed))
    passed = upper(1, width, place, after(top, rows_in), gate_sets[1], filt)
    received.append(lax.ppermute(passed, "section", down))
    sent = rows_in.astype(BF)
    rows_in = [rows_in] + [swap(sent, "section", bit) for bit in (1, 2, 3)]

    parts = [lower(0, width, place, top, after(received[0], passed), gate_sets[0], filt, second)]
    start = after(received[1], parts[0])
    parts.append(lower(1, width, place, top, start, gate_sets[1], filt, second))
    feats = terms(parts, rows_in)
    feats = feats + swap(feats, "section", 1)
    feats = (feats + swap(feats, "section", 2)) + (swap(feats, "section", 4) + swap(feats, "section", 6))
    return feats.reshape(64, 2, 64).transpose(1, 0, 2).reshape(2, 1, 4096)


def solution(mesh):
    in_specs = (
        P("section", None, "dp", None, None),
        P("section", None, "dp", None, None),
        P("section", "dp", None),
        P("section", "dp", None),
        P(None, "dp", None, None),
        P("dp", None),
        P(None, "dp", None),
    )
    return jax.shard_map(shards, mesh=mesh, in_specs=in_specs, out_specs=P(None, "dp", None), check_vma=False)
```
